32 devices in a mesh: parts: 2 (over y), row: 4 (over z), tile: 4 (over x, core).
Axes of the slice: x: 2, y: 2, z: 4, core: 2. Of those that a mesh axis runs over, the one named last changes fastest.
Arguments:
- mismatch: bfloat16 [8, 64, 4096], P(('parts', 'row'), None, 'tile'), parts along dimension 0, may hold values from -6 to 6
- col_weight: bfloat16 [4, 128, 128], P('row'), may hold values from -0.5 to 0.5
- row_weight: bfloat16 [14, 4, 64, 64], P(None, None, 'row'), may hold values from -0.75 to 0.75
- volume: float32 [4, 256, 2048], P('parts', 'row', 'tile'), parts along dimension 0, may hold values from -6 to 6
- step_size: float32 [4], P('parts'), parts along dimension 0, may hold values from 0.1 to 0.4
- combos: int32 [8, 4, 7, 16], P('parts'), parts along dimension 0, may hold values from 0 to 15, each once within a row
- dest_block: int32 [8, 4, 7, 16], P('parts'), parts along dimension 0, may hold values from 0 to 3
- counts: int32 [8, 4, 7, 4], P('parts'), parts along dimension 0, may hold values from 0 to 4, as said below
Outputs:
- volume_next: float32 [4, 256, 2048], P('parts', 'row', 'tile'), parts along dimension 0
The draws below stay inside these ranges and needn't reach their ends.
There are 2 independent parts, one for each index of `parts`. The reference program is written for one: setup_inputs(seed, part) draws one part's arguments, and reference() takes and returns one part's arrays. A program takes and returns all parts, laid end to end along the dimension named above; an argument that names none is the same for every part. Nothing has to cross between parts.
Inputs may be any that keep to these rules, and one draw needn't show every extreme that they name: `combos`: for each source row group, tile group and offset, the last dimension is a permutation of 0 to 15. `counts`: zero where the destination row group g + j - 3 lies outside 0 to 3; at least 4 - abs(j - 3) elsewhere, except where that bound is below zero; in every draw some destination device receives 4 in every bucket from every valid source.
All inputs are finite; a program needn't handle non-finite values.
Results may differ from the reference program's by a relative error of at most 0.0031.
Values may be sent and summed in bfloat16 or wider, within the bound.
A program may use at most 64 MiB of HBM per device.

```python
import math
import jax
import jax.numpy as jnp
from jax import lax

TB = 128
BY = 64
DCOLS = 4096
DR_DEV = 16
NZ = 2
BX = 4
REACH = 3
ANG = 4
DROWS = 64
ROW_GROUPS = 4
TILE_GROUPS = 4
BAND = 7
KINDS = 14
NCT = 8
COMBOS = 16
CAP = 4
VY = 256
VX = 2048


def draw_counts(key, part):
    key = jax.random.fold_in(key, 7)
    subkeys = jax.random.split(key, 3)
    groups = jnp.arange(ROW_GROUPS, dtype=jnp.int32)
    offsets = jnp.arange(BAND, dtype=jnp.int32)
    tile_ids = jnp.arange(TILE_GROUPS, dtype=jnp.int32)
    distance = jnp.abs(offsets - REACH)
    lowest = jnp.maximum(CAP - distance, 0)
    draw_shape = (ROW_GROUPS, TILE_GROUPS, BAND, TILE_GROUPS)
    drawn_counts = jax.random.randint(subkeys[0], draw_shape, lowest[None, None, :, None], CAP + 1, dtype=jnp.int32)
    target_row = groups[:, None, None, None] + offsets[None, None, :, None] - REACH
    inside = (target_row >= 0) & (target_row < ROW_GROUPS)
    full_row = jax.random.randint(subkeys[1], (), 0, ROW_GROUPS, dtype=jnp.int32)
    full_tile = jax.random.randint(subkeys[2], (), 0, TILE_GROUPS, dtype=jnp.int32)
    chosen = (target_row == full_row) & (tile_ids[None, None, None, :] == full_tile)
    drawn_counts = jnp.where(chosen, CAP, drawn_counts)
    return jnp.where(inside, drawn_counts, 0).astype(jnp.int32)


def place_ends(drawn, stream_key, least, high):
    index_at = [jax.random.randint(jax.random.fold_in(stream_key, axis), (), 0, length) for axis, length in enumerate(drawn.shape)]
    widest = drawn.shape.index(max(drawn.shape))
    beside = index_at[:widest] + [(index_at[widest] + 1) % drawn.shape[widest]] + index_at[widest + 1:]
    return drawn.at[tuple(index_at)].set(least).at[tuple(beside)].set(high)


def block_levels(stream_key, shape, cuts, low, top_value):
    level = 1.0
    for axis_at, shards_of in cuts:
        heights = jax.random.uniform(jax.random.fold_in(jax.random.fold_in(stream_key, 6), axis_at), (shards_of,), jnp.float32, low / len(cuts), top_value / len(cuts))
        level = level * jnp.repeat(jnp.exp(heights), shape[axis_at] // shards_of).reshape((-1,) + (1,) * (len(shape) - 1 - axis_at))
    return level


def noise(rng, extent, spread, bound, cuts=(), kind=jnp.bfloat16):
    entries = spread * jax.random.normal(rng, extent, jnp.float32)
    if cuts:
        entries = entries * block_levels(rng, extent, cuts, -0.22, 0.18)
    return jnp.clip(entries, -bound, bound).astype(kind)


def setup_inputs(seed: int = 0, part: int = 0) -> dict:
    keys = jax.random.split(jax.random.key(seed), 9)
    part_keys = jax.random.split(jax.random.fold_in(keys[8], part), 9)
    mismatch = noise(part_keys[0], (ANG, DROWS, DCOLS), 1.0, 6.0, ((0, 4), (2, 4)))
    col_weight = noise(keys[1], (ANG, TB, TB), TB ** -0.5, 0.5, ((0, 4),))
    row_weight = noise(keys[2], (KINDS, ANG, DROWS, BY), (ANG * DR_DEV) ** -0.5, 0.75, ((2, 4),))
    volume = noise(part_keys[3], (NZ, VY, VX), 1.0, 6.0, ((1, 4), (2, 4)), jnp.float32)
    step_size = jnp.clip(jnp.exp(jax.random.uniform(part_keys[4], (NZ,), jnp.float32, math.log(0.1), math.log(0.4))), 0.1, 0.4)
    combos = jax.vmap(lambda own: jax.random.permutation(own, COMBOS))(jax.random.split(part_keys[5], ROW_GROUPS * TILE_GROUPS * BAND)).reshape((ROW_GROUPS, TILE_GROUPS, BAND, COMBOS)).astype(jnp.int32)
    dest_block = place_ends(jax.random.randint(part_keys[6], (ROW_GROUPS, TILE_GROUPS, BAND, COMBOS), 0, BX), jax.random.fold_in(part_keys[6], 1), 0, BX - 1).astype(jnp.int32)
    counts = draw_counts(jax.random.fold_in(jax.random.fold_in(keys[8], part), 71), part)
    return {"mismatch": mismatch, "col_weight": col_weight, "row_weight": row_weight, "volume": volume, "step_size": step_size, "combos": combos, "dest_block": dest_block, "counts": counts}


def reference(mismatch, col_weight, row_weight, volume, step_size, combos, dest_block, counts):
    def filter_angle(pair):
        angle_data, kernel = pair
        local_rows = angle_data.reshape(DROWS, DCOLS // TB, TB).astype(jnp.float32)
        mixed = jnp.einsum("rcv,vu->rcu", local_rows, kernel.astype(jnp.float32))
        return mixed.reshape(DROWS, DCOLS).astype(jnp.bfloat16)

    filtered = lax.map(filter_angle, (mismatch, col_weight))
    combo_depth = combos // NCT
    combo_col = combos % NCT
    slot_tile = jnp.arange(COMBOS, dtype=jnp.int32) // CAP
    slot_index = jnp.arange(COMBOS, dtype=jnp.int32) % CAP
    tile_src = jnp.arange(TILE_GROUPS, dtype=jnp.int32)[:, None, None]
    offset_ids = jnp.arange(BAND, dtype=jnp.int32)

    def add_group(gradient, group):
        rows_here = lax.dynamic_slice_in_dim(filtered, group * DR_DEV, DR_DEV, 1)
        kernels_here = lax.dynamic_slice_in_dim(row_weight, group * DR_DEV, DR_DEV, 2)
        adjoint = jnp.einsum("kary,arc->kyc", kernels_here.astype(jnp.float32), rows_here.astype(jnp.float32))
        adjoint = adjoint.astype(jnp.bfloat16)
        blocks_all = adjoint.reshape(BAND, NZ, BY, TILE_GROUPS, NCT, TB)
        depth_sel = combo_depth[group]
        col_sel = combo_col[group]
        picked = blocks_all[offset_ids[None, :, None], depth_sel, :, tile_src, col_sel, :]
        dest_row = group + offset_ids - REACH
        inside = (dest_row >= 0) & (dest_row < ROW_GROUPS)
        row_safe = jnp.clip(dest_row, 0, ROW_GROUPS - 1)
        group_counts = counts[group][:, :, slot_tile]
        live_slots = (slot_index[None, None, :] < group_counts) & inside[None, :, None]
        dest_col = slot_tile[None, None, :] * BX + dest_block[group]
        contrib = picked.astype(jnp.float32) * live_slots.astype(jnp.float32)[..., None, None]
        gradient = gradient.at[depth_sel, row_safe[None, :, None], :, dest_col, :].add(contrib)
        return gradient, None

    start = jnp.zeros((NZ, ROW_GROUPS, BY, TILE_GROUPS * BX, TB), jnp.float32)
    gradient, unused = lax.scan(add_group, start, jnp.arange(ROW_GROUPS, dtype=jnp.int32))
    gradient = gradient.reshape(NZ, VY, VX)
    return volume - step_size[:, None, None] * gradient
```

```python
import functools

import jax
import jax.numpy as jnp
from jax import lax
from jax.experimental import pallas as pl
from jax.experimental.pallas import tpu as pltpu
from jax.sharding import PartitionSpec as P

MESH = pl.DeviceIdType.MESH


def near_first(rows):
    orders = [sorted(range(rows), key=lambda a: (abs(a - me), a)) for me in range(rows)]
    return [sum(orders[me][k] * rows**me for me in range(rows)) for k in range(rows)]


def kernel(
    rows, tiles, reach, mis_ref, cw_ref, rw_ref, combos_ref, dest_ref, counts_ref, out_ref,
    filt, work, weights, mask, picked, total, part_out, part_in,
    w_send, w_recv, f_send, f_recv, p_send, p_recv, own_sem,
):
    me = lax.axis_index("row")
    tile = lax.axis_index("tile")
    edge = cw_ref.shape[0]
    col_blocks = mis_ref.shape[1] // edge
    depth = out_ref.shape[0]
    group_rows = rw_ref.shape[2]
    bx = out_ref.shape[2] // edge
    cap = combos_ref.shape[3] // tiles

    barrier = pltpu.get_barrier_semaphore()
    for d in range(1, rows):
        pl.semaphore_signal(barrier, inc=1, device_id={"row": lax.rem(me + d, rows)}, device_id_type=MESH)
    for d in range(1, tiles):
        pl.semaphore_signal(barrier, inc=1, device_id={"tile": lax.rem(tile + d, tiles)}, device_id_type=MESH)

    for c in range(col_blocks):
        filt[me, c] = jnp.dot(
            mis_ref[:, c * edge:(c + 1) * edge], cw_ref[...], preferred_element_type=jnp.float32
        ).astype(jnp.bfloat16)
    own_w = pltpu.make_async_copy(rw_ref.at[pl.ds(depth * reach, depth)], weights.at[me], own_sem)
    own_w.start()
    pl.semaphore_wait(barrier, rows + tiles - 2)

    codes = near_first(rows)
    scale = jnp.int32(1)
    for i in range(1, rows):
        scale = scale * (1 + (rows - 1) * ((me + rows - i) // rows))
    order = [(jnp.int32(code) // scale) % rows for code in codes]

    w_copies, f_copies = [], []
    for k in range(1, rows):
        peer = order[k]
        w_copies.append(pltpu.make_async_remote_copy(
            src_ref=rw_ref.at[pl.ds(depth * (peer - me + reach), depth)],
            dst_ref=weights.at[me],
            send_sem=w_send.at[peer], recv_sem=w_recv.at[me],
            device_id={"row": peer}, device_id_type=MESH,
        ))
        w_copies[-1].start()
    for k in range(1, rows):
        peer = order[k]
        f_copies.append(pltpu.make_async_remote_copy(
            src_ref=filt.at[me], dst_ref=filt.at[me],
            send_sem=f_send.at[peer], recv_sem=f_recv.at[me],
            device_id={"row": peer}, device_id_type=MESH,
        ))
        f_copies[-1].start()

    def fill(i, carry):
        g, q = i // (tiles * cap), i % (tiles * cap)
        j = me - g + reach
        m = combos_ref[g, tile, j, q]
        place = (m // col_blocks) * bx + dest_ref[g, tile, j, q]
        live = (q % cap) < counts_ref[g, tile, j, q // cap]
        code = jnp.where(live, place, -1)
        for n in range(depth * bx):
            mask[i, n] = jnp.full(mask.shape[2:], jnp.where(code == n, 1.0, 0.0), jnp.float32).astype(jnp.bfloat16)
        return carry

    lax.fori_loop(0, rows * tiles * cap, fill, 0)

    own_w.wait()
    for k in range(1, rows):
        src = order[k]
        pltpu.make_async_remote_copy(
            src_ref=rw_ref.at[pl.ds(0, depth)], dst_ref=weights.at[src],
            send_sem=w_send.at[src], recv_sem=w_recv.at[src],
            device_id={"row": src}, device_id_type=MESH,
        ).wait_recv()

    def term(a, t):
        def group(g, carry):
            at = pl.ds(pl.multiple_of(g * group_rows, group_rows), group_rows)
            j = me - g + reach
            slots = [(g * tiles + t) * cap + s for s in range(cap)]
            blocks = [
                work[combos_ref[g, tile, j, t * cap + s] % col_blocks, at, :] for s in range(cap)
            ]
            for n in range(depth * bx):
                value = mask[slots[0], n] * blocks[0]
                for s in range(1, cap):
                    value = value + mask[slots[s], n] * blocks[s]
                picked[n // bx, at, (n % bx) * edge:(n % bx + 1) * edge] = value
            return carry

        lax.fori_loop(0, rows, group, 0)
        sums = []
        for z in range(depth):
            w = weights[:, z, pl.ds(a, 1), :, :].reshape(rows * group_rows, weights.shape[4])
            sums.append(lax.dot_general(
                w, picked[z], (((0,), (0,)), ((), ())), preferred_element_type=jnp.float32
            ))
        return sums

    for k in range(rows - 1):
        a = order[k]
        if k:
            pltpu.make_async_remote_copy(
                src_ref=filt.at[a], dst_ref=filt.at[a],
                send_sem=f_send.at[a], recv_sem=f_recv.at[a],
                device_id={"row": a}, device_id_type=MESH,
            ).wait_recv()

        work[...] = filt[a]

        def add(t, carry, a=a, k=k):
            for z, s in enumerate(term(a, t)):
                if k:
                    total[t, z] += s
                else:
                    total[t, z] = s
            return carry

        lax.fori_loop(0, tiles, add, 0)

    a = order[rows - 1]
    pltpu.make_async_remote_copy(
        src_ref=filt.at[a], dst_ref=filt.at[a],
        send_sem=f_send.at[a], recv_sem=f_recv.at[a],
        device_id={"row": a}, device_id_type=MESH,
    ).wait_recv()
    work[...] = filt[a]
    pair = tile // 2
    peers = []
    for m in range(1, tiles // 2):
        other = lax.rem(pair + m, tiles // 2)
        peers += [other * 2 + tile % 2, other * 2 + 1 - tile % 2]
    peers.append(pair * 2 + 1 - tile % 2)
    p_copies = []
    for t in peers:
        for z, s in enumerate(term(a, t)):
            part_out[t, z] = (total[t, z] + s).astype(jnp.bfloat16)
        p_copies.append(pltpu.make_async_remote_copy(
            src_ref=part_out.at[t], dst_ref=part_in.at[tile],
            send_sem=p_send.at[t], recv_sem=p_recv.at[tile],
            device_id={"tile": t}, device_id_type=MESH,
        ))
        p_copies[-1].start()
    for z, s in enumerate(term(a, tile)):
        out_ref[z] = total[tile, z] + s
    for t in reversed(peers):
        pltpu.make_async_remote_copy(
            src_ref=part_out.at[t], dst_ref=part_in.at[t],
            send_sem=p_send.at[t], recv_sem=p_recv.at[t],
            device_id={"tile": t}, device_id_type=MESH,
        ).wait_recv()
        for z in range(depth):
            out_ref[z] += part_in[t, z].astype(jnp.float32)
    for copy in w_copies + f_copies + p_copies:
        copy.wait_send()


def gather_rows(rows, tiles, mismatch, col_weight, row_weight, volume, step_size, combos, dest_block, counts):
    det_rows, det_cols = mismatch.shape[1:]
    edge = col_weight.shape[1]
    kinds, angles, group_rows, block_rows = row_weight.shape
    depth = volume.shape[0]
    reach = kinds // depth // 2
    bx = volume.shape[2] // edge
    cap = combos.shape[3] // tiles
    bf16 = jnp.bfloat16
    vmem, smem = pl.BlockSpec(memory_space=pltpu.VMEM), pl.BlockSpec(memory_space=pltpu.SMEM)
    dma = pltpu.SemaphoreType.DMA
    gradient = pl.pallas_call(
        functools.partial(kernel, rows, tiles, reach),
        out_shape=jax.ShapeDtypeStruct(volume.shape, jnp.float32),
        in_specs=[vmem] * 3 + [smem] * 3,
        out_specs=vmem,
        scratch_shapes=[
            pltpu.VMEM((rows, det_cols // edge, det_rows, edge), bf16),
            pltpu.VMEM((det_cols // edge, det_rows, edge), bf16),
            pltpu.VMEM((rows, depth, angles, group_rows, block_rows), bf16),
            pltpu.VMEM((rows * tiles * cap, depth * bx, group_rows, edge), bf16),
            pltpu.VMEM((depth, det_rows, bx * edge), bf16),
            pltpu.VMEM((tiles,) + volume.shape, jnp.float32),
            pltpu.VMEM((tiles,) + volume.shape, bf16),
            pltpu.VMEM((tiles,) + volume.shape, bf16),
            dma((rows,)), dma((rows,)), dma((rows,)), dma((rows,)), dma((tiles,)), dma((tiles,)), dma,
        ],
        compiler_params=pltpu.CompilerParams(
            collective_id=0, has_side_effects=True, vmem_limit_bytes=32 * 2**20
        ),
    )(mismatch[0], col_weight[0], row_weight, combos, dest_block, counts)
    return volume - step_size[:, None, None] * gradient


def shifted(shard, axis, by):
    length = lax.axis_size(axis)
    pairs = [(i, i + by) for i in range(length) if 0 <= i + by < length]
    return lax.ppermute(shard, axis, pairs)


def per_device(mismatch, col_weight, row_weight, volume, step_size, combos, dest_block, counts):
    ang_dev, det_rows, det_cols = mismatch.shape
    tile_edge = col_weight.shape[1]
    block_rows = row_weight.shape[3]
    col_blocks = det_cols // tile_edge
    depth_layers = volume.shape[0]
    voxel_blocks = volume.shape[2] // tile_edge
    band_width = row_weight.shape[0] // depth_layers
    reach_rows = band_width // 2
    tile_count = lax.axis_size("tile")
    row_count = lax.axis_size("row")
    slot_cap = combos.shape[3] // tile_count
    row_index = lax.axis_index("row")
    tile_index = lax.axis_index("tile")
    filtered = jnp.einsum(
        "arcv,avu->arcu",
        mismatch.reshape(ang_dev, det_rows, col_blocks, tile_edge),
        col_weight,
        preferred_element_type=jnp.float32,
    )
    filtered = filtered.astype(jnp.bfloat16).reshape(ang_dev, det_rows, det_cols)
    adjoint = jnp.einsum(
        "kary,arc->kyc",
        row_weight,
        lax.all_to_all(filtered, "row", split_axis=1, concat_axis=0, tiled=True),
        preferred_element_type=jnp.float32,
    ).astype(jnp.bfloat16)
    blocks_all = adjoint.reshape(band_width, depth_layers, block_rows, col_blocks, tile_edge)
    own_combo = combos[row_index, tile_index]
    offsets = jnp.arange(band_width, dtype=jnp.int32)[:, None]
    outgoing = blocks_all[offsets, own_combo // col_blocks, :, own_combo % col_blocks, :]
    outgoing = outgoing.reshape(band_width, tile_count, slot_cap, block_rows, tile_edge)
    pieces = [
        lax.all_to_all(
            shifted(outgoing[offset], "row", offset - reach_rows),
            "tile",
            split_axis=0,
            concat_axis=0,
            tiled=True,
        )
        for offset in range(band_width)
    ]
    incoming = jnp.stack(pieces)
    offset_ids = jnp.arange(band_width, dtype=jnp.int32)
    source_rows = row_index - (offset_ids - reach_rows)
    inside = (source_rows >= 0) & (source_rows < row_count)
    source_safe = jnp.clip(source_rows, 0, row_count - 1)
    tile_ids = jnp.arange(tile_count, dtype=jnp.int32)
    slot_ids = jnp.arange(slot_cap, dtype=jnp.int32)
    slot_cols = tile_index * slot_cap + slot_ids
    arriving = combos[
        source_safe[:, None, None],
        tile_ids[None, :, None],
        offset_ids[:, None, None],
        slot_cols[None, None, :],
    ]
    arriving_dest = dest_block[
        source_safe[:, None, None],
        tile_ids[None, :, None],
        offset_ids[:, None, None],
        slot_cols[None, None, :],
    ]
    arriving_count = counts[
        source_safe[:, None], tile_ids[None, :], offset_ids[:, None], tile_index
    ]
    live_slots = inside[:, None, None] & (slot_ids[None, None, :] < arriving_count[:, :, None])
    target = arriving // col_blocks * voxel_blocks + arriving_dest
    places = jnp.arange(depth_layers * voxel_blocks, dtype=jnp.int32)
    selector = ((target[..., None] == places) & live_slots[..., None]).astype(jnp.bfloat16)
    total_slots = band_width * tile_count * slot_cap
    selector = selector.reshape(total_slots, depth_layers, voxel_blocks)
    gradient = jnp.einsum(
        "szb,syx->zybx",
        selector,
        incoming.reshape(total_slots, block_rows, tile_edge),
        preferred_element_type=jnp.float32,
    )
    gradient = gradient.reshape(depth_layers, block_rows, voxel_blocks * tile_edge)
    return volume - step_size[:, None, None] * gradient


def solution(mesh):
    rows, tiles = mesh.shape["row"], mesh.shape["tile"]

    def body(mismatch, col_weight, row_weight, volume, *rest):
        reach = row_weight.shape[0] // volume.shape[0] // 2
        near = 1 < rows <= reach + 1 and tiles % 2 == 0 and mismatch.shape[0] == 1
        run = functools.partial(gather_rows, rows, tiles) if near else per_device
        return run(mismatch, col_weight, row_weight, volume, *rest)

    return jax.shard_map(
        body,
        mesh=mesh,
        in_specs=(
            P(("parts", "row"), None, "tile"),
            P("row", None, None),
            P(None, None, "row", None),
            P("parts", "row", "tile"),
            P("parts"),
            P("parts", None, None, None),
            P("parts", None, None, None),
            P("parts", None, None, None),
        ),
        out_specs=P("parts", "row", "tile"),
        check_vma=False,
    )
```

```python
import functools

import jax
import jax.numpy as jnp
from jax import lax
from jax.experimental import pallas as pl
from jax.experimental.pallas import tpu as pltpu
from jax.sharding import PartitionSpec as P

MESH = pl.DeviceIdType.MESH


def near_first(rows):
    orders = [sorted(range(rows), key=lambda a: (abs(a - me), a)) for me in range(rows)]
    return [sum(orders[me][k] * rows**me for me in range(rows)) for k in range(rows)]


def kernel(
    rows, tiles, reach, mis_hbm, cw_hbm, rw_hbm, combos_hbm, dest_hbm, counts_hbm, out_ref,
    mis_ref, cw_ref, rw_ref, combos_ref, dest_ref, counts_ref,
    filt, work, packed, weights, mask, picked, total, part_out, part_in,
    in_sem, rw_sem, int_sem, w_send, w_recv, f_send, f_recv, p_send, p_recv,
):
    me = lax.axis_index("row")
    tile = lax.axis_index("tile")
    edge = cw_ref.shape[0]
    col_blocks = mis_ref.shape[1] // edge
    depth = out_ref.shape[0]
    group_rows, block_rows = rw_ref.shape[3:]
    bx = out_ref.shape[2] // edge
    cap = combos_ref.shape[2] // tiles
    halves = f_send.shape[2]
    half = col_blocks // halves

    barrier = pltpu.get_barrier_semaphore()
    for d in range(1, rows):
        pl.semaphore_signal(barrier, inc=1, device_id={"row": lax.rem(me + d, rows)}, device_id_type=MESH)
    for d in range(1, tiles):
        pl.semaphore_signal(barrier, inc=1, device_id={"tile": lax.rem(tile + d, tiles)}, device_id_type=MESH)

    loads = [
        pltpu.make_async_copy(mis_hbm, mis_ref, in_sem.at[0]),
        pltpu.make_async_copy(cw_hbm, cw_ref, in_sem.at[1]),
    ]
    w_loads = [
        pltpu.make_async_copy(rw_hbm.at[pl.ds(depth * (r - me + reach), depth)], rw_ref.at[r], rw_sem.at[r])
        for r in range(rows)
    ]
    int_loads = []
    for g in range(rows):
        j = me - g + reach
        int_loads += [
            pltpu.make_async_copy(combos_hbm.at[g, j], combos_ref.at[g], int_sem.at[0, g]),
            pltpu.make_async_copy(dest_hbm.at[g, j], dest_ref.at[g], int_sem.at[1, g]),
            pltpu.make_async_copy(counts_hbm.at[g, tile], counts_ref.at[g], int_sem.at[2, g]),
        ]
    for copy in loads + w_loads + int_loads:
        copy.start()

    codes = near_first(rows)
    scale = jnp.int32(1)
    for i in range(1, rows):
        scale = scale * (1 + (rows - 1) * ((me + rows - i) // rows))
    order = [(jnp.int32(code) // scale) % rows for code in codes]

    for copy in loads:
        copy.wait()
    for c in range(col_blocks):
        filt[me, c] = jnp.dot(
            mis_ref[:, c * edge:(c + 1) * edge], cw_ref[...], preferred_element_type=jnp.float32
        ).astype(jnp.bfloat16)
    for r in range(rows):
        w_loads[r].wait()
        packed[r] = jnp.concatenate([rw_ref[r, z] for z in range(depth)], axis=-1)
    weights[me] = packed[me]
    pl.semaphore_wait(barrier, rows + tiles - 2)

    def w_copy(k):
        peer = order[k]
        return pltpu.make_async_remote_copy(
            src_ref=packed.at[peer], dst_ref=weights.at[me],
            send_sem=w_send.at[peer], recv_sem=w_recv.at[me],
            device_id={"row": peer}, device_id_type=MESH,
        )

    def f_copy(a, side, h):
        return pltpu.make_async_remote_copy(
            src_ref=filt.at[a, pl.ds(h * half, half)], dst_ref=filt.at[a, pl.ds(h * half, half)],
            send_sem=f_send.at[a, side, h], recv_sem=f_recv.at[a, h],
            device_id={"row": lax.rem(me + rows - 1 + 2 * side, rows)}, device_id_type=MESH,
        )

    def goes(a, side):
        if side:
            return jnp.logical_and(a <= me, me + 1 < rows)
        return jnp.logical_and(a >= me, me > 0)

    def forward(a, h):
        for side in range(2):
            @pl.when(goes(a, side))
            def _():
                f_copy(a, side, h).start()

    for k in range(1, rows):
        w_copy(k).start()
    for h in range(halves):
        forward(me, h)

    for copy in int_loads:
        copy.wait()

    def fill(i, carry):
        g, q = i // (tiles * cap), i % (tiles * cap)
        place = (combos_ref[g, tile, q] // col_blocks) * bx + dest_ref[g, tile, q]
        live = (q % cap) < counts_ref[g, q // cap, me - g + reach]
        code = jnp.where(live, place, -1)
        for n in range(depth * bx):
            mask[i, n] = jnp.full(mask.shape[2:], jnp.where(code == n, 1.0, 0.0), jnp.float32).astype(jnp.bfloat16)
        return carry

    lax.fori_loop(0, rows * tiles * cap, fill, 0)

    for k in range(1, rows):
        src = order[k]
        pltpu.make_async_remote_copy(
            src_ref=packed.at[src], dst_ref=weights.at[src],
            send_sem=w_send.at[src], recv_sem=w_recv.at[src],
            device_id={"row": src}, device_id_type=MESH,
        ).wait_recv()

    def term(a, t):
        def group(g, carry):
            at = pl.ds(pl.multiple_of(g * group_rows, group_rows), group_rows)
            slots = [(g * tiles + t) * cap + s for s in range(cap)]
            blocks = [work[combos_ref[g, tile, t * cap + s] % col_blocks, at, :] for s in range(cap)]
            for n in range(depth * bx):
                value = mask[slots[0], n] * blocks[0]
                for s in range(1, cap):
                    value = value + mask[slots[s], n] * blocks[s]
                picked[n // bx, at, (n % bx) * edge:(n % bx + 1) * edge] = value
            return carry

        lax.fori_loop(0, rows, group, 0)
        w = weights[:, pl.ds(a, 1), :, :].reshape(rows * group_rows, weights.shape[3])
        return [
            lax.dot_general(
                w[:, z * block_rows:(z + 1) * block_rows], picked[z],
                (((0,), (0,)), ((), ())), preferred_element_type=jnp.float32,
            )
            for z in range(depth)
        ]

    def accumulate(k):
        a = order[k]
        work[...] = filt[a]

        def add(t, carry):
            for z, s in enumerate(term(a, t)):
                if k:
                    total[t, z] += s
                else:
                    total[t, z] = s
            return carry

        lax.fori_loop(0, tiles, add, 0)

    def arrive(k):
        a = order[k]
        for h in range(halves):
            f_copy(a, 0, h).wait_recv()
            forward(a, h)

    accumulate(0)
    waiting = []
    for k in range(1, rows - 1):
        arrive(k)
        waiting.append(k)
        if k % 2 == 0 or k == rows - 2:
            for w in waiting:
                accumulate(w)
            waiting = []
    arrive(rows - 1)
    a = order[rows - 1]
    work[...] = filt[a]
    pair = tile // 2
    peers = []
    for m in range(1, tiles // 2):
        other = lax.rem(pair + m, tiles // 2)
        peers += [other * 2 + tile % 2, other * 2 + 1 - tile % 2]
    peers.append(pair * 2 + 1 - tile % 2)
    p_copies = []
    for t in peers:
        for z, s in enumerate(term(a, t)):
            part_out[t, z] = (total[t, z] + s).astype(jnp.bfloat16)
        p_copies.append(pltpu.make_async_remote_copy(
            src_ref=part_out.at[t], dst_ref=part_in.at[tile],
            send_sem=p_send.at[t], recv_sem=p_recv.at[tile],
            device_id={"tile": t}, device_id_type=MESH,
        ))
        p_copies[-1].start()
    for z, s in enumerate(term(a, tile)):
        out_ref[z] = total[tile, z] + s
    for t in reversed(peers):
        pltpu.make_async_remote_copy(
            src_ref=part_out.at[t], dst_ref=part_in.at[t],
            send_sem=p_send.at[t], recv_sem=p_recv.at[t],
            device_id={"tile": t}, device_id_type=MESH,
        ).wait_recv()
        for z in range(depth):
            out_ref[z] += part_in[t, z].astype(jnp.float32)
    for k in range(1, rows):
        w_copy(k).wait_send()
    for a in range(rows):
        for side in range(2):
            @pl.when(goes(a, side))
            def _():
                for h in range(halves):
                    f_copy(a, side, h).wait_send()
    for copy in p_copies:
        copy.wait_send()


def gather_rows(rows, tiles, mismatch, col_weight, row_weight, volume, step_size, combos, dest_block, counts):
    det_rows, det_cols = mismatch.shape[1:]
    edge = col_weight.shape[1]
    kinds, angles, group_rows, block_rows = row_weight.shape
    depth = volume.shape[0]
    band = kinds // depth
    bx = volume.shape[2] // edge
    cap = combos.shape[3] // tiles
    col_blocks = det_cols // edge
    halves = 2 - col_blocks % 2
    bf16 = jnp.bfloat16
    hbm, dma = pl.BlockSpec(memory_space=pltpu.HBM), pltpu.SemaphoreType.DMA
    gradient = pl.pallas_call(
        functools.partial(kernel, rows, tiles, band // 2),
        out_shape=jax.ShapeDtypeStruct(volume.shape, jnp.float32),
        in_specs=[hbm] * 6,
        out_specs=pl.BlockSpec(memory_space=pltpu.VMEM),
        scratch_shapes=[
            pltpu.VMEM((det_rows, det_cols), bf16),
            pltpu.VMEM((edge, edge), bf16),
            pltpu.VMEM((rows, depth, angles, group_rows, block_rows), bf16),
            pltpu.SMEM((rows, tiles, combos.shape[3]), jnp.int32),
            pltpu.SMEM((rows, tiles, combos.shape[3]), jnp.int32),
            pltpu.SMEM((rows, tiles, band), jnp.int32),
            pltpu.VMEM((rows, col_blocks, det_rows, edge), bf16),
            pltpu.VMEM((col_blocks, det_rows, edge), bf16),
            pltpu.VMEM((rows, angles, group_rows, depth * block_rows), bf16),
            pltpu.VMEM((rows, angles, group_rows, depth * block_rows), bf16),
            pltpu.VMEM((rows * tiles * cap, depth * bx, group_rows, edge), bf16),
            pltpu.VMEM((depth, det_rows, bx * edge), bf16),
            pltpu.VMEM((tiles,) + volume.shape, jnp.float32),
            pltpu.VMEM((tiles,) + volume.shape, bf16),
            pltpu.VMEM((tiles,) + volume.shape, bf16),
            dma((2,)), dma((rows,)), dma((3, rows)), dma((rows,)), dma((rows,)),
            dma((rows, 2, halves)), dma((rows, halves)), dma((tiles,)), dma((tiles,)),
        ],
        compiler_params=pltpu.CompilerParams(
            collective_id=0, has_side_effects=True, vmem_limit_bytes=63 * 2**20
        ),
    )(
        mismatch[0], col_weight[0], row_weight,
        combos.transpose(0, 2, 1, 3), dest_block.transpose(0, 2, 1, 3), counts.transpose(0, 1, 3, 2),
    )
    return volume - step_size[:, None, None] * gradient


def shifted(shard, axis, by):
    length = lax.axis_size(axis)
    pairs = [(i, i + by) for i in range(length) if 0 <= i + by < length]
    return lax.ppermute(shard, axis, pairs)


def per_device(mismatch, col_weight, row_weight, volume, step_size, combos, dest_block, counts):
    ang_dev, det_rows, det_cols = mismatch.shape
    tile_edge = col_weight.shape[1]
    block_rows = row_weight.shape[3]
    col_blocks = det_cols // tile_edge
    depth_layers = volume.shape[0]
    voxel_blocks = volume.shape[2] // tile_edge
    band_width = row_weight.shape[0] // depth_layers
    reach_rows = band_width // 2
    tile_count = lax.axis_size("tile")
    row_count = lax.axis_size("row")
    slot_cap = combos.shape[3] // tile_count
    row_index = lax.axis_index("row")
    tile_index = lax.axis_index("tile")
    filtered = jnp.einsum(
        "arcv,avu->arcu",
        mismatch.reshape(ang_dev, det_rows, col_blocks, tile_edge),
        col_weight,
        preferred_element_type=jnp.float32,
    )
    filtered = filtered.astype(jnp.bfloat16).reshape(ang_dev, det_rows, det_cols)
    adjoint = jnp.einsum(
        "kary,arc->kyc",
        row_weight,
        lax.all_to_all(filtered, "row", split_axis=1, concat_axis=0, tiled=True),
        preferred_element_type=jnp.float32,
    ).astype(jnp.bfloat16)
    blocks_all = adjoint.reshape(band_width, depth_layers, block_rows, col_blocks, tile_edge)
    own_combo = combos[row_index, tile_index]
    offsets = jnp.arange(band_width, dtype=jnp.int32)[:, None]
    outgoing = blocks_all[offsets, own_combo // col_blocks, :, own_combo % col_blocks, :]
    outgoing = outgoing.reshape(band_width, tile_count, slot_cap, block_rows, tile_edge)
    pieces = [
        lax.all_to_all(
            shifted(outgoing[offset], "row", offset - reach_rows),
            "tile",
            split_axis=0,
            concat_axis=0,
            tiled=True,
        )
        for offset in range(band_width)
    ]
    incoming = jnp.stack(pieces)
    offset_ids = jnp.arange(band_width, dtype=jnp.int32)
    source_rows = row_index - (offset_ids - reach_rows)
    inside = (source_rows >= 0) & (source_rows < row_count)
    source_safe = jnp.clip(source_rows, 0, row_count - 1)
    tile_ids = jnp.arange(tile_count, dtype=jnp.int32)
    slot_ids = jnp.arange(slot_cap, dtype=jnp.int32)
    slot_cols = tile_index * slot_cap + slot_ids
    arriving = combos[
        source_safe[:, None, None],
        tile_ids[None, :, None],
        offset_ids[:, None, None],
        slot_cols[None, None, :],
    ]
    arriving_dest = dest_block[
        source_safe[:, None, None],
        tile_ids[None, :, None],
        offset_ids[:, None, None],
        slot_cols[None, None, :],
    ]
    arriving_count = counts[
        source_safe[:, None], tile_ids[None, :], offset_ids[:, None], tile_index
    ]
    live_slots = inside[:, None, None] & (slot_ids[None, None, :] < arriving_count[:, :, None])
    target = arriving // col_blocks * voxel_blocks + arriving_dest
    places = jnp.arange(depth_layers * voxel_blocks, dtype=jnp.int32)
    selector = ((target[..., None] == places) & live_slots[..., None]).astype(jnp.bfloat16)
    total_slots = band_width * tile_count * slot_cap
    selector = selector.reshape(total_slots, depth_layers, voxel_blocks)
    gradient = jnp.einsum(
        "szb,syx->zybx",
        selector,
        incoming.reshape(total_slots, block_rows, tile_edge),
        preferred_element_type=jnp.float32,
    )
    gradient = gradient.reshape(depth_layers, block_rows, voxel_blocks * tile_edge)
    return volume - step_size[:, None, None] * gradient


def solution(mesh):
    rows, tiles = mesh.shape["row"], mesh.shape["tile"]

    def body(mismatch, col_weight, row_weight, volume, *rest):
        reach = row_weight.shape[0] // volume.shape[0] // 2
        near = 1 < rows <= reach + 1 and tiles % 2 == 0 and mismatch.shape[0] == 1
        run = functools.partial(gather_rows, rows, tiles) if near else per_device
        return run(mismatch, col_weight, row_weight, volume, *rest)

    return jax.shard_map(
        body,
        mesh=mesh,
        in_specs=(
            P(("parts", "row"), None, "tile"),
            P("row", None, None),
            P(None, None, "row", None),
            P("parts", "row", "tile"),
            P("parts"),
            P("parts", None, None, None),
            P("parts", None, None, None),
            P("parts", None, None, None),
        ),
        out_specs=P("parts", "row", "tile"),
        check_vma=False,
    )
```

```python
import functools

import jax
import jax.numpy as jnp
from jax import lax
from jax.experimental import pallas as pl
from jax.experimental.pallas import tpu as pltpu
from jax.sharding import PartitionSpec as P

MESH = pl.DeviceIdType.MESH


def near_first(rows):
    orders = [sorted(range(rows), key=lambda a: (abs(a - me), a)) for me in range(rows)]
    return [sum(orders[me][k] * rows**me for me in range(rows)) for k in range(rows)]


def kernel(
    rows, tiles, reach, mis_hbm, cw_hbm, rw_hbm, combos_hbm, dest_hbm, counts_hbm, vol_hbm, step_hbm, out_ref,
    mis_ref, cw_ref, rw_ref, combos_ref, dest_ref, counts_ref, vol_ref, step_ref,
    filt, work, packed, weights, mask, picked, total,
    in_sem, rw_sem, int_sem, w_send, w_recv, z_send, x_send, s_send, f_recv,
):
    me = lax.axis_index("row")
    tile = lax.axis_index("tile")
    edge = cw_ref.shape[0]
    col_blocks = mis_ref.shape[1] // edge
    depth = out_ref.shape[0]
    group_rows, block_rows = rw_ref.shape[3:]
    bx = out_ref.shape[2] // edge
    cap = combos_ref.shape[2] // tiles
    halves = f_recv.shape[2]
    half = col_blocks // halves

    barrier = pltpu.get_barrier_semaphore()
    for d in range(1, rows):
        pl.semaphore_signal(barrier, inc=1, device_id={"row": lax.rem(me + d, rows)}, device_id_type=MESH)
    pairs = tiles // 2
    core = tile % 2
    sibling = tile + 1 - 2 * core
    mirrors = [lax.rem(tile // 2 + m, pairs) * 2 + core for m in range(1, pairs)]
    for t in [sibling] + mirrors:
        pl.semaphore_signal(barrier, inc=1, device_id={"tile": t}, device_id_type=MESH)

    loads = [
        pltpu.make_async_copy(mis_hbm, mis_ref, in_sem.at[0]),
        pltpu.make_async_copy(cw_hbm, cw_ref, in_sem.at[1]),
    ]
    w_loads = [
        pltpu.make_async_copy(rw_hbm.at[pl.ds(depth * (r - me + reach), depth)], rw_ref.at[r], rw_sem.at[r])
        for r in range(rows)
    ]
    int_loads = []
    for g in range(rows):
        j = me - g + reach
        int_loads += [
            pltpu.make_async_copy(combos_hbm.at[g, j], combos_ref.at[g], int_sem.at[0, g]),
            pltpu.make_async_copy(dest_hbm.at[g, j], dest_ref.at[g], int_sem.at[1, g]),
            pltpu.make_async_copy(counts_hbm.at[g], counts_ref.at[g], int_sem.at[2, g]),
        ]
    late_loads = [
        pltpu.make_async_copy(vol_hbm, vol_ref, in_sem.at[2]),
        pltpu.make_async_copy(step_hbm, step_ref, in_sem.at[3]),
    ]
    for copy in loads + w_loads + int_loads + late_loads:
        copy.start()

    codes = near_first(rows)
    scale = jnp.int32(1)
    for i in range(1, rows):
        scale = scale * (1 + (rows - 1) * ((me + rows - i) // rows))
    order = [(jnp.int32(code) // scale) % rows for code in codes]

    for copy in loads:
        copy.wait()
    for c in range(col_blocks):
        filt[tile, me, c] = jnp.dot(
            mis_ref[:, c * edge:(c + 1) * edge], cw_ref[...], preferred_element_type=jnp.float32
        ).astype(jnp.bfloat16)
    for r in range(rows):
        w_loads[r].wait()
        packed[r] = jnp.concatenate([rw_ref[r, z] for z in range(depth)], axis=-1)
    weights[me] = packed[me]
    pl.semaphore_wait(barrier, rows + pairs - 1)

    def w_copy(k):
        peer = order[k]
        return pltpu.make_async_remote_copy(
            src_ref=packed.at[peer], dst_ref=weights.at[me],
            send_sem=w_send.at[peer], recv_sem=w_recv.at[me],
            device_id={"row": peer}, device_id_type=MESH,
        )

    def f_copy(t, a, h, sem, to):
        piece = filt.at[t, a, pl.ds(h * half, half)]
        return pltpu.make_async_remote_copy(
            src_ref=piece, dst_ref=piece, send_sem=sem, recv_sem=f_recv.at[t, a, h],
            device_id=to, device_id_type=MESH,
        )

    def z_copy(a, side, h):
        return f_copy(tile, a, h, z_send.at[a, side, h], {"row": lax.rem(me + rows - 1 + 2 * side, rows)})

    def x_copies(a, h):
        return [f_copy(tile, a, h, x_send.at[m, a, h], {"tile": t}) for m, t in enumerate(mirrors)]

    def s_copy(t, a, h):
        return f_copy(t, a, h, s_send.at[t, a, h], {"tile": sibling})

    def wait_piece(t, a, h):
        s_copy(t, a, h).wait_recv()

    def goes(a, side):
        if side:
            return jnp.logical_and(a <= me, me + 1 < rows)
        return jnp.logical_and(a >= me, me > 0)

    def forward(a, h):
        for side in range(2):
            @pl.when(goes(a, side))
            def _():
                z_copy(a, side, h).start()

        for copy in x_copies(a, h) + [s_copy(tile, a, h)]:
            copy.start()

    for h in range(halves):
        forward(me, h)
    for k in range(1, rows):
        w_copy(k).start()

    for copy in int_loads:
        copy.wait()

    def fill(i, carry):
        g, t, s = i // (tiles * cap), i // cap % tiles, i % cap
        place = (combos_ref[g, t, tile * cap + s] // col_blocks) * bx + dest_ref[g, t, tile * cap + s]
        live = s < counts_ref[g, t, tile, me - g + reach]
        code = jnp.where(live, place, -1)
        for n in range(depth * bx):
            mask[i, n] = jnp.full(mask.shape[2:], jnp.where(code == n, 1.0, 0.0), jnp.float32).astype(jnp.bfloat16)
        return carry

    lax.fori_loop(0, rows * tiles * cap, fill, 0)

    def weights_in():
        for k in range(1, rows):
            src = order[k]
            pltpu.make_async_remote_copy(
                src_ref=packed.at[src], dst_ref=weights.at[src],
                send_sem=w_send.at[src], recv_sem=w_recv.at[src],
                device_id={"row": src}, device_id_type=MESH,
            ).wait_recv()

    def accumulate(k):
        a = order[k]
        for t in range(tiles):
            work[t] = filt[t, a]

        def group(g, carry):
            at = pl.ds(pl.multiple_of(g * group_rows, group_rows), group_rows)
            sums = [None] * (depth * bx)
            for t in range(tiles):
                slots = [(g * tiles + t) * cap + s for s in range(cap)]
                blocks = [
                    work[t, combos_ref[g, t, tile * cap + s] % col_blocks, at, :] for s in range(cap)
                ]
                for n in range(depth * bx):
                    value = mask[slots[0], n] * blocks[0]
                    for s in range(1, cap):
                        value = value + mask[slots[s], n] * blocks[s]
                    value = value.astype(jnp.float32)
                    sums[n] = value if t == 0 else sums[n] + value
            for n in range(depth * bx):
                picked[n // bx, at, (n % bx) * edge:(n % bx + 1) * edge] = sums[n].astype(jnp.bfloat16)
            return carry

        lax.fori_loop(0, rows, group, 0)
        w = weights[:, pl.ds(a, 1), :, :].reshape(rows * group_rows, weights.shape[3])
        for z in range(depth):
            value = lax.dot_general(
                w[:, z * block_rows:(z + 1) * block_rows], picked[z],
                (((0,), (0,)), ((), ())), preferred_element_type=jnp.float32,
            )
            if k:
                value = total[z] + value
            if k < rows - 1:
                total[z] = value
            else:
                out_ref[z] = vol_ref[z] - step_ref[z] * value

    for k in range(1, rows):
        for h in range(halves):
            wait_piece(tile, order[k], h)
            forward(order[k], h)
    for k in range(rows):
        for h in range(halves):
            for t in mirrors:
                wait_piece(t, order[k], h)
                s_copy(t, order[k], h).start()
        if k == rows - 1:
            for copy in late_loads:
                copy.wait()
        for p in range(pairs):
            for h in range(halves):
                if k:
                    wait_piece(p * 2 + 1 - core, order[k - 1], h)
        if k == 1:
            weights_in()
        if k:
            accumulate(k - 1)
    for p in range(pairs):
        for h in range(halves):
            wait_piece(p * 2 + 1 - core, order[rows - 1], h)
    accumulate(rows - 1)
    for k in range(1, rows):
        w_copy(k).wait_send()
    for a in range(rows):
        for side in range(2):
            @pl.when(goes(a, side))
            def _():
                for h in range(halves):
                    z_copy(a, side, h).wait_send()
        for h in range(halves):
            for copy in x_copies(a, h):
                copy.wait_send()
            for t in [tile] + mirrors:
                s_copy(t, a, h).wait_send()


def gather_rows(rows, tiles, mismatch, col_weight, row_weight, volume, step_size, combos, dest_block, counts):
    det_rows, det_cols = mismatch.shape[1:]
    edge = col_weight.shape[1]
    kinds, angles, group_rows, block_rows = row_weight.shape
    depth = volume.shape[0]
    band = kinds // depth
    bx = volume.shape[2] // edge
    cap = combos.shape[3] // tiles
    col_blocks = det_cols // edge
    halves = 2 - col_blocks % 2
    bf16 = jnp.bfloat16
    hbm, dma = pl.BlockSpec(memory_space=pltpu.HBM), pltpu.SemaphoreType.DMA
    return pl.pallas_call(
        functools.partial(kernel, rows, tiles, band // 2),
        out_shape=jax.ShapeDtypeStruct(volume.shape, jnp.float32),
        in_specs=[hbm] * 8,
        out_specs=pl.BlockSpec(memory_space=pltpu.VMEM),
        scratch_shapes=[
            pltpu.VMEM((det_rows, det_cols), bf16),
            pltpu.VMEM((edge, edge), bf16),
            pltpu.VMEM((rows, depth, angles, group_rows, block_rows), bf16),
            pltpu.SMEM((rows, tiles, combos.shape[3]), jnp.int32),
            pltpu.SMEM((rows, tiles, combos.shape[3]), jnp.int32),
            pltpu.SMEM((rows, tiles, tiles, band), jnp.int32),
            pltpu.VMEM(volume.shape, jnp.float32),
            pltpu.SMEM(step_size.shape, jnp.float32),
            pltpu.VMEM((tiles, rows, col_blocks, det_rows, edge), bf16),
            pltpu.VMEM((tiles, col_blocks, det_rows, edge), bf16),
            pltpu.VMEM((rows, angles, group_rows, depth * block_rows), bf16),
            pltpu.VMEM((rows, angles, group_rows, depth * block_rows), bf16),
            pltpu.VMEM((rows * tiles * cap, depth * bx, group_rows, edge), bf16),
            pltpu.VMEM((depth, det_rows, bx * edge), bf16),
            pltpu.VMEM(volume.shape, jnp.float32),
            dma((4,)), dma((rows,)), dma((3, rows)), dma((rows,)), dma((rows,)),
            dma((rows, 2, halves)), dma((tiles // 2, rows, halves)), dma((tiles, rows, halves)),
            dma((tiles, rows, halves)),
        ],
        compiler_params=pltpu.CompilerParams(
            collective_id=0, has_side_effects=True, vmem_limit_bytes=63 * 2**20
        ),
    )(
        mismatch[0], col_weight[0], row_weight,
        combos.transpose(0, 2, 1, 3), dest_block.transpose(0, 2, 1, 3), counts.transpose(0, 1, 3, 2),
        volume, step_size,
    )


def shifted(shard, axis, by):
    length = lax.axis_size(axis)
    pairs = [(i, i + by) for i in range(length) if 0 <= i + by < length]
    return lax.ppermute(shard, axis, pairs)


def per_device(mismatch, col_weight, row_weight, volume, step_size, combos, dest_block, counts):
    ang_dev, det_rows, det_cols = mismatch.shape
    tile_edge = col_weight.shape[1]
    block_rows = row_weight.shape[3]
    col_blocks = det_cols // tile_edge
    depth_layers = volume.shape[0]
    voxel_blocks = volume.shape[2] // tile_edge
    band_width = row_weight.shape[0] // depth_layers
    reach_rows = band_width // 2
    tile_count = lax.axis_size("tile")
    row_count = lax.axis_size("row")
    slot_cap = combos.shape[3] // tile_count
    row_index = lax.axis_index("row")
    tile_index = lax.axis_index("tile")
    filtered = jnp.einsum(
        "arcv,avu->arcu",
        mismatch.reshape(ang_dev, det_rows, col_blocks, tile_edge),
        col_weight,
        preferred_element_type=jnp.float32,
    )
    filtered = filtered.astype(jnp.bfloat16).reshape(ang_dev, det_rows, det_cols)
    adjoint = jnp.einsum(
        "kary,arc->kyc",
        row_weight,
        lax.all_to_all(filtered, "row", split_axis=1, concat_axis=0, tiled=True),
        preferred_element_type=jnp.float32,
    ).astype(jnp.bfloat16)
    blocks_all = adjoint.reshape(band_width, depth_layers, block_rows, col_blocks, tile_edge)
    own_combo = combos[row_index, tile_index]
    offsets = jnp.arange(band_width, dtype=jnp.int32)[:, None]
    outgoing = blocks_all[offsets, own_combo // col_blocks, :, own_combo % col_blocks, :]
    outgoing = outgoing.reshape(band_width, tile_count, slot_cap, block_rows, tile_edge)
    pieces = [
        lax.all_to_all(
            shifted(outgoing[offset], "row", offset - reach_rows),
            "tile",
            split_axis=0,
            concat_axis=0,
            tiled=True,
        )
        for offset in range(band_width)
    ]
    incoming = jnp.stack(pieces)
    offset_ids = jnp.arange(band_width, dtype=jnp.int32)
    source_rows = row_index - (offset_ids - reach_rows)
    inside = (source_rows >= 0) & (source_rows < row_count)
    source_safe = jnp.clip(source_rows, 0, row_count - 1)
    tile_ids = jnp.arange(tile_count, dtype=jnp.int32)
    slot_ids = jnp.arange(slot_cap, dtype=jnp.int32)
    slot_cols = tile_index * slot_cap + slot_ids
    arriving = combos[
        source_safe[:, None, None],
        tile_ids[None, :, None],
        offset_ids[:, None, None],
        slot_cols[None, None, :],
    ]
    arriving_dest = dest_block[
        source_safe[:, None, None],
        tile_ids[None, :, None],
        offset_ids[:, None, None],
        slot_cols[None, None, :],
    ]
    arriving_count = counts[
        source_safe[:, None], tile_ids[None, :], offset_ids[:, None], tile_index
    ]
    live_slots = inside[:, None, None] & (slot_ids[None, None, :] < arriving_count[:, :, None])
    target = arriving // col_blocks * voxel_blocks + arriving_dest
    places = jnp.arange(depth_layers * voxel_blocks, dtype=jnp.int32)
    selector = ((target[..., None] == places) & live_slots[..., None]).astype(jnp.bfloat16)
    total_slots = band_width * tile_count * slot_cap
    selector = selector.reshape(total_slots, depth_layers, voxel_blocks)
    gradient = jnp.einsum(
        "szb,syx->zybx",
        selector,
        incoming.reshape(total_slots, block_rows, tile_edge),
        preferred_element_type=jnp.float32,
    )
    gradient = gradient.reshape(depth_layers, block_rows, voxel_blocks * tile_edge)
    return volume - step_size[:, None, None] * gradient


def solution(mesh):
    rows, tiles = mesh.shape["row"], mesh.shape["tile"]

    def body(mismatch, col_weight, row_weight, volume, *rest):
        reach = row_weight.shape[0] // volume.shape[0] // 2
        near = 1 < rows <= reach + 1 and tiles % 2 == 0 and mismatch.shape[0] == 1
        run = functools.partial(gather_rows, rows, tiles) if near else per_device
        return run(mismatch, col_weight, row_weight, volume, *rest)

    return jax.shard_map(
        body,
        mesh=mesh,
        in_specs=(
            P(("parts", "row"), None, "tile"),
            P("row", None, None),
            P(None, None, "row", None),
            P("parts", "row", "tile"),
            P("parts"),
            P("parts", None, None, None),
            P("parts", None, None, None),
            P("parts", None, None, None),
        ),
        out_specs=P("parts", "row", "tile"),
        check_vma=False,
    )
```

```python
import functools

import jax
import jax.numpy as jnp
from jax import lax
from jax.experimental import pallas as pl
from jax.experimental.pallas import tpu as pltpu
from jax.sharding import PartitionSpec as P

MESH = pl.DeviceIdType.MESH


def near_first(rows):
    orders = [sorted(range(rows), key=lambda a: (abs(a - me), a)) for me in range(rows)]
    return [sum(orders[me][k] * rows**me for me in range(rows)) for k in range(rows)]


def kernel(
    rows, tiles, reach, mis_hbm, cw_hbm, rw_hbm, combos_hbm, dest_hbm, counts_hbm, vol_hbm, step_hbm, out_ref,
    mis_ref, cw_ref, rw_ref, combos_ref, dest_ref, counts_ref, vol_ref, step_ref,
    filt, work, packed, weights, mask, picked, total,
    in_sem, rw_sem, int_sem, w_send, w_recv, z_send, x_send, s_send, f_recv,
):
    me = lax.axis_index("row")
    tile = lax.axis_index("tile")
    edge = cw_ref.shape[0]
    col_blocks = mis_ref.shape[1] // edge
    depth = out_ref.shape[0]
    group_rows, block_rows = rw_ref.shape[3:]
    bx = out_ref.shape[2] // edge
    cap = combos_ref.shape[2] // tiles
    halves = f_recv.shape[2]
    half = col_blocks // halves

    barrier = pltpu.get_barrier_semaphore()
    for d in range(1, rows):
        pl.semaphore_signal(barrier, inc=1, device_id={"row": lax.rem(me + d, rows)}, device_id_type=MESH)
    pairs = tiles // 2
    core = tile % 2
    sibling = tile + 1 - 2 * core
    mirrors = [lax.rem(tile // 2 + m, pairs) * 2 + core for m in range(1, pairs)]
    for t in [sibling] + mirrors:
        pl.semaphore_signal(barrier, inc=1, device_id={"tile": t}, device_id_type=MESH)

    loads = [
        pltpu.make_async_copy(mis_hbm, mis_ref, in_sem.at[0]),
        pltpu.make_async_copy(cw_hbm, cw_ref, in_sem.at[1]),
    ]
    w_loads = [
        pltpu.make_async_copy(rw_hbm.at[pl.ds(depth * (r - me + reach), depth)], rw_ref.at[r], rw_sem.at[r])
        for r in range(rows)
    ]
    int_loads = []
    for g in range(rows):
        j = me - g + reach
        int_loads += [
            pltpu.make_async_copy(combos_hbm.at[g, j], combos_ref.at[g], int_sem.at[0, g]),
            pltpu.make_async_copy(dest_hbm.at[g, j], dest_ref.at[g], int_sem.at[1, g]),
            pltpu.make_async_copy(counts_hbm.at[g], counts_ref.at[g], int_sem.at[2, g]),
        ]
    late_loads = [
        pltpu.make_async_copy(vol_hbm, vol_ref, in_sem.at[2]),
        pltpu.make_async_copy(step_hbm, step_ref, in_sem.at[3]),
    ]
    for copy in loads + w_loads + int_loads + late_loads:
        copy.start()

    codes = near_first(rows)
    scale = jnp.int32(1)
    for i in range(1, rows):
        scale = scale * (1 + (rows - 1) * ((me + rows - i) // rows))
    order = [(jnp.int32(code) // scale) % rows for code in codes]

    for copy in loads:
        copy.wait()
    for c in range(col_blocks):
        filt[tile, me, c] = jnp.dot(
            mis_ref[:, c * edge:(c + 1) * edge], cw_ref[...], preferred_element_type=jnp.float32
        ).astype(jnp.bfloat16)
    pl.semaphore_wait(barrier, rows + pairs - 1)

    def w_copy(k):
        peer = order[k]
        return pltpu.make_async_remote_copy(
            src_ref=packed.at[peer], dst_ref=weights.at[me],
            send_sem=w_send.at[peer], recv_sem=w_recv.at[me],
            device_id={"row": peer}, device_id_type=MESH,
        )

    def f_copy(t, a, h, sem, to):
        piece = filt.at[t, a, pl.ds(h * half, half)]
        return pltpu.make_async_remote_copy(
            src_ref=piece, dst_ref=piece, send_sem=sem, recv_sem=f_recv.at[t, a, h],
            device_id=to, device_id_type=MESH,
        )

    def z_copy(a, side, h):
        return f_copy(tile, a, h, z_send.at[a, side, h], {"row": lax.rem(me + rows - 1 + 2 * side, rows)})

    def x_copies(a, h):
        return [f_copy(tile, a, h, x_send.at[m, a, h], {"tile": t}) for m, t in enumerate(mirrors)]

    def s_copy(t, a, h):
        return f_copy(t, a, h, s_send.at[t, a, h], {"tile": sibling})

    def wait_piece(t, a, h):
        s_copy(t, a, h).wait_recv()

    def goes(a, side):
        if side:
            return jnp.logical_and(a <= me, me + 1 < rows)
        return jnp.logical_and(a >= me, me > 0)

    def forward(a, h):
        for side in range(2):
            @pl.when(goes(a, side))
            def _():
                z_copy(a, side, h).start()

        for copy in x_copies(a, h) + [s_copy(tile, a, h)]:
            copy.start()

    for h in range(halves):
        forward(me, h)
    for r in range(rows):
        w_loads[r].wait()
        packed[r] = jnp.concatenate([rw_ref[r, z] for z in range(depth)], axis=-1)
    weights[me] = packed[me]
    for k in range(1, rows):
        w_copy(k).start()

    for copy in int_loads:
        copy.wait()

    def fill(i, carry):
        g, t, s = i // (tiles * cap), i // cap % tiles, i % cap
        place = (combos_ref[g, t, tile * cap + s] // col_blocks) * bx + dest_ref[g, t, tile * cap + s]
        live = s < counts_ref[g, t, tile, me - g + reach]
        code = jnp.where(live, place, -1)
        for n in range(depth * bx):
            mask[i, n] = jnp.full(mask.shape[2:], jnp.where(code == n, 1.0, 0.0), jnp.float32).astype(jnp.bfloat16)
        return carry

    lax.fori_loop(0, rows * tiles * cap, fill, 0)

    def weights_in():
        for k in range(1, rows):
            src = order[k]
            pltpu.make_async_remote_copy(
                src_ref=packed.at[src], dst_ref=weights.at[src],
                send_sem=w_send.at[src], recv_sem=w_recv.at[src],
                device_id={"row": src}, device_id_type=MESH,
            ).wait_recv()

    def accumulate(k):
        a = order[k]
        for t in range(tiles):
            work[t] = filt[t, a]

        def group(g, carry):
            at = pl.ds(pl.multiple_of(g * group_rows, group_rows), group_rows)
            sums = [None] * (depth * bx)
            for t in range(tiles):
                slots = [(g * tiles + t) * cap + s for s in range(cap)]
                blocks = [
                    work[t, combos_ref[g, t, tile * cap + s] % col_blocks, at, :] for s in range(cap)
                ]
                for n in range(depth * bx):
                    value = mask[slots[0], n] * blocks[0]
                    for s in range(1, cap):
                        value = value + mask[slots[s], n] * blocks[s]
                    value = value.astype(jnp.float32)
                    sums[n] = value if t == 0 else sums[n] + value
            for n in range(depth * bx):
                picked[n // bx, at, (n % bx) * edge:(n % bx + 1) * edge] = sums[n].astype(jnp.bfloat16)
            return carry

        lax.fori_loop(0, rows, group, 0)
        w = weights[:, pl.ds(a, 1), :, :].reshape(rows * group_rows, weights.shape[3])
        for z in range(depth):
            value = lax.dot_general(
                w[:, z * block_rows:(z + 1) * block_rows], picked[z],
                (((0,), (0,)), ((), ())), preferred_element_type=jnp.float32,
            )
            if k:
                value = total[z] + value
            if k < rows - 1:
                total[z] = value
            else:
                out_ref[z] = vol_ref[z] - step_ref[z] * value

    for k in range(1, rows):
        for h in range(halves):
            wait_piece(tile, order[k], h)
            forward(order[k], h)
    for k in range(rows):
        for h in range(halves):
            for t in mirrors:
                wait_piece(t, order[k], h)
                s_copy(t, order[k], h).start()
        if k == rows - 1:
            for copy in late_loads:
                copy.wait()
        for p in range(pairs):
            for h in range(halves):
                if k:
                    wait_piece(p * 2 + 1 - core, order[k - 1], h)
        if k == 1:
            weights_in()
        if k:
            accumulate(k - 1)
    for p in range(pairs):
        for h in range(halves):
            wait_piece(p * 2 + 1 - core, order[rows - 1], h)
    accumulate(rows - 1)
    for k in range(1, rows):
        w_copy(k).wait_send()
    for a in range(rows):
        for side in range(2):
            @pl.when(goes(a, side))
            def _():
                for h in range(halves):
                    z_copy(a, side, h).wait_send()
        for h in range(halves):
            for copy in x_copies(a, h):
                copy.wait_send()
            for t in [tile] + mirrors:
                s_copy(t, a, h).wait_send()


def gather_rows(rows, tiles, mismatch, col_weight, row_weight, volume, step_size, combos, dest_block, counts):
    det_rows, det_cols = mismatch.shape[1:]
    edge = col_weight.shape[1]
    kinds, angles, group_rows, block_rows = row_weight.shape
    depth = volume.shape[0]
    band = kinds // depth
    bx = volume.shape[2] // edge
    cap = combos.shape[3] // tiles
    col_blocks = det_cols // edge
    halves = 2 - col_blocks % 2
    bf16 = jnp.bfloat16
    hbm, dma = pl.BlockSpec(memory_space=pltpu.HBM), pltpu.SemaphoreType.DMA
    return pl.pallas_call(
        functools.partial(kernel, rows, tiles, band // 2),
        out_shape=jax.ShapeDtypeStruct(volume.shape, jnp.float32),
        in_specs=[hbm] * 8,
        out_specs=pl.BlockSpec(memory_space=pltpu.VMEM),
        scratch_shapes=[
            pltpu.VMEM((det_rows, det_cols), bf16),
            pltpu.VMEM((edge, edge), bf16),
            pltpu.VMEM((rows, depth, angles, group_rows, block_rows), bf16),
            pltpu.SMEM((rows, tiles, combos.shape[3]), jnp.int32),
            pltpu.SMEM((rows, tiles, combos.shape[3]), jnp.int32),
            pltpu.SMEM((rows, tiles, tiles, band), jnp.int32),
            pltpu.VMEM(volume.shape, jnp.float32),
            pltpu.SMEM(step_size.shape, jnp.float32),
            pltpu.VMEM((tiles, rows, col_blocks, det_rows, edge), bf16),
            pltpu.VMEM((tiles, col_blocks, det_rows, edge), bf16),
            pltpu.VMEM((rows, angles, group_rows, depth * block_rows), bf16),
            pltpu.VMEM((rows, angles, group_rows, depth * block_rows), bf16),
            pltpu.VMEM((rows * tiles * cap, depth * bx, group_rows, edge), bf16),
            pltpu.VMEM((depth, det_rows, bx * edge), bf16),
            pltpu.VMEM(volume.shape, jnp.float32),
            dma((4,)), dma((rows,)), dma((3, rows)), dma((rows,)), dma((rows,)),
            dma((rows, 2, halves)), dma((tiles // 2, rows, halves)), dma((tiles, rows, halves)),
            dma((tiles, rows, halves)),
        ],
        compiler_params=pltpu.CompilerParams(
            collective_id=0, has_side_effects=True, vmem_limit_bytes=32 * 2**20
        ),
    )(*(pltpu.with_memory_space_constraint(x, pltpu.HBM) for x in (
        mismatch[0], col_weight[0], row_weight,
        combos.transpose(0, 2, 1, 3), dest_block.transpose(0, 2, 1, 3), counts.transpose(0, 1, 3, 2),
        volume, step_size,
    )))


def shifted(shard, axis, by):
    length = lax.axis_size(axis)
    pairs = [(i, i + by) for i in range(length) if 0 <= i + by < length]
    return lax.ppermute(shard, axis, pairs)


def per_device(mismatch, col_weight, row_weight, volume, step_size, combos, dest_block, counts):
    ang_dev, det_rows, det_cols = mismatch.shape
    tile_edge = col_weight.shape[1]
    block_rows = row_weight.shape[3]
    col_blocks = det_cols // tile_edge
    depth_layers = volume.shape[0]
    voxel_blocks = volume.shape[2] // tile_edge
    band_width = row_weight.shape[0] // depth_layers
    reach_rows = band_width // 2
    tile_count = lax.axis_size("tile")
    row_count = lax.axis_size("row")
    slot_cap = combos.shape[3] // tile_count
    row_index = lax.axis_index("row")
    tile_index = lax.axis_index("tile")
    filtered = jnp.einsum(
        "arcv,avu->arcu",
        mismatch.reshape(ang_dev, det_rows, col_blocks, tile_edge),
        col_weight,
        preferred_element_type=jnp.float32,
    )
    filtered = filtered.astype(jnp.bfloat16).reshape(ang_dev, det_rows, det_cols)
    adjoint = jnp.einsum(
        "kary,arc->kyc",
        row_weight,
        lax.all_to_all(filtered, "row", split_axis=1, concat_axis=0, tiled=True),
        preferred_element_type=jnp.float32,
    ).astype(jnp.bfloat16)
    blocks_all = adjoint.reshape(band_width, depth_layers, block_rows, col_blocks, tile_edge)
    own_combo = combos[row_index, tile_index]
    offsets = jnp.arange(band_width, dtype=jnp.int32)[:, None]
    outgoing = blocks_all[offsets, own_combo // col_blocks, :, own_combo % col_blocks, :]
    outgoing = outgoing.reshape(band_width, tile_count, slot_cap, block_rows, tile_edge)
    pieces = [
        lax.all_to_all(
            shifted(outgoing[offset], "row", offset - reach_rows),
            "tile",
            split_axis=0,
            concat_axis=0,
            tiled=True,
        )
        for offset in range(band_width)
    ]
    incoming = jnp.stack(pieces)
    offset_ids = jnp.arange(band_width, dtype=jnp.int32)
    source_rows = row_index - (offset_ids - reach_rows)
    inside = (source_rows >= 0) & (source_rows < row_count)
    source_safe = jnp.clip(source_rows, 0, row_count - 1)
    tile_ids = jnp.arange(tile_count, dtype=jnp.int32)
    slot_ids = jnp.arange(slot_cap, dtype=jnp.int32)
    slot_cols = tile_index * slot_cap + slot_ids
    arriving = combos[
        source_safe[:, None, None],
        tile_ids[None, :, None],
        offset_ids[:, None, None],
        slot_cols[None, None, :],
    ]
    arriving_dest = dest_block[
        source_safe[:, None, None],
        tile_ids[None, :, None],
        offset_ids[:, None, None],
        slot_cols[None, None, :],
    ]
    arriving_count = counts[
        source_safe[:, None], tile_ids[None, :], offset_ids[:, None], tile_index
    ]
    live_slots = inside[:, None, None] & (slot_ids[None, None, :] < arriving_count[:, :, None])
    target = arriving // col_blocks * voxel_blocks + arriving_dest
    places = jnp.arange(depth_layers * voxel_blocks, dtype=jnp.int32)
    selector = ((target[..., None] == places) & live_slots[..., None]).astype(jnp.bfloat16)
    total_slots = band_width * tile_count * slot_cap
    selector = selector.reshape(total_slots, depth_layers, voxel_blocks)
    gradient = jnp.einsum(
        "szb,syx->zybx",
        selector,
        incoming.reshape(total_slots, block_rows, tile_edge),
        preferred_element_type=jnp.float32,
    )
    gradient = gradient.reshape(depth_layers, block_rows, voxel_blocks * tile_edge)
    return volume - step_size[:, None, None] * gradient


def solution(mesh):
    rows, tiles = mesh.shape["row"], mesh.shape["tile"]

    def body(mismatch, col_weight, row_weight, volume, *rest):
        reach = row_weight.shape[0] // volume.shape[0] // 2
        near = 1 < rows <= reach + 1 and tiles % 2 == 0 and mismatch.shape[0] == 1
        run = functools.partial(gather_rows, rows, tiles) if near else per_device
        return run(mismatch, col_weight, row_weight, volume, *rest)

    return jax.shard_map(
        body,
        mesh=mesh,
        in_specs=(
            P(("parts", "row"), None, "tile"),
            P("row", None, None),
            P(None, None, "row", None),
            P("parts", "row", "tile"),
            P("parts"),
            P("parts", None, None, None),
            P("parts", None, None, None),
            P("parts", None, None, None),
        ),
        out_specs=P("parts", "row", "tile"),
        check_vma=False,
    )
```
